32 devices in a mesh: dp: 2 (over y), tm: 16 (over z, x, core).
Axes of the slice: x: 2, y: 2, z: 4, core: 2. Of those that a mesh axis runs over, the one named last changes fastest.
Arguments:
- query_proj: bfloat16 [2, 2048, 768], P('dp', 'tm'), may hold values from -240 to 240
- key_proj: bfloat16 [2, 2048, 768], P('dp', 'tm'), may hold values from -6 to 6
- value_proj: bfloat16 [2, 2048, 768], P('dp', 'tm'), may hold values from -6 to 6
- cotangent: bfloat16 [2, 2048, 768], P('dp', 'tm'), may hold values from -6 to 6
- lengths: int32 [2], P('dp'), may hold values from 1024 to 2048, as said below
- rel_bias: float32 [12, 257], replicated, may hold values from -4 to 4
Outputs:
- context: bfloat16 [2, 2048, 768], P('dp', 'tm')
- grad_query: bfloat16 [2, 2048, 768], P('dp', 'tm')
- grad_key: bfloat16 [2, 2048, 768], P('dp', 'tm')
- grad_value: bfloat16 [2, 2048, 768], P('dp', 'tm')
- grad_bias: float32 [12, 257], replicated
The draws below stay inside these ranges and needn't reach their ends.
Inputs may be any that keep to these rules, and one draw needn't show every extreme that they name: `lengths`: one utterance has all 2048 frames valid and another exactly 1024.
All inputs are finite; a program needn't handle non-finite values.
Results may differ from the reference program's by a relative error of at most 0.005.
Values may be sent and summed in bfloat16 or wider, within the bound.
A program may use at most 64 MiB of HBM per device.

```python
import jax
import jax.numpy as jnp
from jax import lax

H = 12
HD = 64
W = 128
F = 128
D = 768
BATCH = 2
FRAMES = 2048
N_TM = 16


def drawn_pair(key):
    array_shape = (BATCH, FRAMES, D)
    key_drawn = jnp.clip(jax.random.normal(jax.random.fold_in(key, 21), array_shape, jnp.float32), -6.0, 6.0)
    query_drawn = jnp.clip(jax.random.normal(jax.random.fold_in(key, 22), array_shape, jnp.float32), -6.0, 6.0)
    return (query_drawn, key_drawn)


def draw_query_proj(key, part):
    return drawn_pair(key)[0].astype(jnp.bfloat16)


def draw_key_proj(key, part):
    return drawn_pair(key)[1].astype(jnp.bfloat16)


def draw_lengths(key, part):
    drawn = jax.random.randint(jax.random.fold_in(key, 11), (BATCH,), FRAMES // 2, FRAMES + 1)
    longest = jax.random.randint(jax.random.fold_in(key, 12), (), 0, BATCH)
    shortest = (longest + 1 + jax.random.randint(jax.random.fold_in(key, 13), (), 0, BATCH - 1)) % BATCH
    positions = jnp.arange(BATCH)
    drawn = jnp.where(positions == longest, FRAMES, drawn)
    drawn = jnp.where(positions == shortest, FRAMES // 2, drawn)
    return drawn.astype(jnp.int32)


def block_scale(own_key, shape, shards, low, largest):
    def one(axis_at, parts):
        heights = jax.random.uniform(jax.random.fold_in(jax.random.fold_in(own_key, 6), axis_at), (parts,), jnp.float32, low / len(shards), largest / len(shards))
        return jnp.repeat(jnp.exp(heights), shape[axis_at] // parts).reshape((-1,) + (1,) * (len(shape) - axis_at - 1))

    loudness = one(*shards[0])
    for cut in shards[1:]:
        loudness = loudness * one(*cut)
    return loudness


def noise(rng, shape, spread, limit, shards=(), kind=jnp.bfloat16):
    level = block_scale(rng, shape, shards, -0.22, 0.18) if shards else 1.0
    entries = jax.random.normal(rng, shape, jnp.float32) * spread * level
    return jnp.minimum(jnp.maximum(entries, -limit), limit).astype(kind)


def setup_inputs(seed: int = 0) -> dict:
    seeds = jax.random.split(jax.random.key(seed), 7)
    return {
        "query_proj": draw_query_proj(jax.random.fold_in(seeds[6], 71), 0),
        "key_proj": draw_key_proj(jax.random.fold_in(seeds[6], 71), 0),
        "value_proj": noise(seeds[2], (BATCH, FRAMES, D), 1.0, 6.0, ((0, 2), (1, 16))),
        "cotangent": noise(seeds[3], (BATCH, FRAMES, D), 1.0, 6.0, ((0, 2), (1, 16))),
        "lengths": draw_lengths(jax.random.fold_in(seeds[6], 71), 0),
        "rel_bias": noise(seeds[5], (H, 2 * W + 1), 1.0, 4.0, (), jnp.float32),
    }


masked_score = -1e30


def band_matrix(bias_table, height, breadth):
    num_heads = bias_table.shape[0]
    span_cols = bias_table.shape[1]
    repeated = jnp.broadcast_to(bias_table[:, None, :], (num_heads, height, span_cols))
    padded = jnp.pad(repeated, ((0, 0), (0, 0), (0, breadth + 1 - span_cols)))
    flattened = padded.reshape(num_heads, height * (breadth + 1))[:, : height * breadth]
    return flattened.reshape(num_heads, height, breadth)


def band_sum(values, span_cols):
    num_heads, height, breadth = values.shape
    flattened = jnp.pad(values.reshape(num_heads, height * breadth), ((0, 0), (0, height)))
    return jnp.sum(flattened.reshape(num_heads, height, breadth + 1)[:, :, :span_cols], axis=1)


def query_side(query_rows, key_rows, value_rows, grad_rows, bias_table, query_pos, key_pos, length):
    scaling = HD ** -0.5
    height = query_rows.shape[0]
    breadth = key_rows.shape[0]
    scores = jnp.einsum("qhd,khd->hqk", query_rows.astype(jnp.float32), key_rows.astype(jnp.float32)) * scaling
    scores = scores + band_matrix(bias_table, height, breadth)
    allowed = (jnp.abs(key_pos[None, :] - query_pos[:, None]) <= W) & (key_pos[None, :] >= 0) & (key_pos[None, :] < length)
    scores = jnp.where(allowed[None], scores, masked_score)
    row_max = jnp.max(scores, axis=-1)
    shifted = jnp.exp(scores - row_max[..., None])
    row_total = jnp.sum(shifted, axis=-1)
    log_total = row_max + jnp.log(row_total)
    attn_probs = shifted / row_total[..., None]
    valid_rows = query_pos < length
    probs_low = attn_probs.astype(jnp.bfloat16)
    mixed = jnp.einsum("hqk,khd->qhd", probs_low.astype(jnp.float32), value_rows.astype(jnp.float32))
    context = jnp.where(valid_rows[:, None, None], mixed, 0.0).astype(jnp.bfloat16)
    masked_grad = jnp.where(valid_rows[:, None, None], grad_rows, jnp.zeros_like(grad_rows))
    grad_probs = jnp.einsum("qhd,khd->hqk", masked_grad.astype(jnp.float32), value_rows.astype(jnp.float32))
    row_delta = jnp.sum(attn_probs * grad_probs, axis=-1)
    grad_scores = attn_probs * (grad_probs - row_delta[..., None])
    grad_low = grad_scores.astype(jnp.bfloat16)
    grad_query = (jnp.einsum("hqk,khd->qhd", grad_low.astype(jnp.float32), key_rows.astype(jnp.float32)) * scaling).astype(jnp.bfloat16)
    grad_table = band_sum(grad_scores, bias_table.shape[1])
    return context, grad_query, log_total, row_delta, grad_table


def key_side(key_rows, value_rows, query_rows, grad_rows, log_total, row_delta, bias_table, key_pos, query_pos, length):
    scaling = HD ** -0.5
    height = key_rows.shape[0]
    breadth = query_rows.shape[0]
    scores = jnp.einsum("khd,qhd->hkq", key_rows.astype(jnp.float32), query_rows.astype(jnp.float32)) * scaling
    scores = scores + band_matrix(bias_table[:, ::-1], height, breadth)
    valid_query = (query_pos >= 0) & (query_pos < length)
    allowed = (jnp.abs(query_pos[None, :] - key_pos[:, None]) <= W) & (key_pos[:, None] < length) & valid_query[None, :]
    attn_probs = jnp.where(allowed[None], jnp.exp(jnp.where(allowed[None], scores - log_total[:, None, :], 0.0)), 0.0)
    probs_low = attn_probs.astype(jnp.bfloat16)
    masked_grad = jnp.where(valid_query[:, None, None], grad_rows, jnp.zeros_like(grad_rows))
    grad_probs = jnp.einsum("khd,qhd->hkq", value_rows.astype(jnp.float32), masked_grad.astype(jnp.float32))
    grad_scores = attn_probs * (grad_probs - row_delta[:, None, :])
    grad_low = grad_scores.astype(jnp.bfloat16)
    grad_key = jnp.einsum("hkq,qhd->khd", grad_low.astype(jnp.float32), query_rows.astype(jnp.float32)) * scaling
    grad_value = jnp.einsum("hkq,qhd->khd", probs_low.astype(jnp.float32), masked_grad.astype(jnp.float32))
    return grad_key.astype(jnp.bfloat16), grad_value.astype(jnp.bfloat16)


def reference(query_proj, key_proj, value_proj, cotangent, lengths, rel_bias):
    extended = F + 2 * W
    blocks = BATCH * N_TM
    rim_pad = ((0, 0), (W, W), (0, 0))
    key_padded = jnp.pad(key_proj, rim_pad)
    value_padded = jnp.pad(value_proj, rim_pad)
    query_padded = jnp.pad(query_proj, rim_pad)
    grad_padded = jnp.pad(cotangent, rim_pad)
    zero_index = jnp.zeros((), jnp.int32)

    def forward_block(block_index):
        utterance = (block_index // N_TM).astype(jnp.int32)
        first_frame = ((block_index % N_TM) * F).astype(jnp.int32)
        length = lengths[utterance]
        query_rows = lax.dynamic_slice(query_proj, (utterance, first_frame, zero_index), (1, F, D))[0].reshape(F, H, HD)
        grad_rows = lax.dynamic_slice(cotangent, (utterance, first_frame, zero_index), (1, F, D))[0].reshape(F, H, HD)
        key_rows = lax.dynamic_slice(key_padded, (utterance, first_frame, zero_index), (1, extended, D))[0].reshape(extended, H, HD)
        value_rows = lax.dynamic_slice(value_padded, (utterance, first_frame, zero_index), (1, extended, D))[0].reshape(extended, H, HD)
        query_pos = first_frame + jnp.arange(F, dtype=jnp.int32)
        key_pos = first_frame - W + jnp.arange(extended, dtype=jnp.int32)
        return query_side(query_rows, key_rows, value_rows, grad_rows, rel_bias, query_pos, key_pos, length)

    context, grad_query, log_total, row_delta, grad_tables = lax.map(forward_block, jnp.arange(blocks, dtype=jnp.int32))
    context = context.reshape(BATCH, FRAMES, D)
    grad_query = grad_query.reshape(BATCH, FRAMES, D)
    grad_bias = jnp.sum(grad_tables, axis=0)
    log_total = jnp.pad(log_total.reshape(BATCH, N_TM, H, F).transpose(0, 2, 1, 3).reshape(BATCH, H, FRAMES), ((0, 0), (0, 0), (W, W)))
    row_delta = jnp.pad(row_delta.reshape(BATCH, N_TM, H, F).transpose(0, 2, 1, 3).reshape(BATCH, H, FRAMES), ((0, 0), (0, 0), (W, W)))

    def keyside_block(block_index):
        utterance = (block_index // N_TM).astype(jnp.int32)
        first_frame = ((block_index % N_TM) * F).astype(jnp.int32)
        length = lengths[utterance]
        key_rows = lax.dynamic_slice(key_proj, (utterance, first_frame, zero_index), (1, F, D))[0].reshape(F, H, HD)
        value_rows = lax.dynamic_slice(value_proj, (utterance, first_frame, zero_index), (1, F, D))[0].reshape(F, H, HD)
        query_rows = lax.dynamic_slice(query_padded, (utterance, first_frame, zero_index), (1, extended, D))[0].reshape(extended, H, HD)
        grad_rows = lax.dynamic_slice(grad_padded, (utterance, first_frame, zero_index), (1, extended, D))[0].reshape(extended, H, HD)
        total_rows = lax.dynamic_slice(log_total, (utterance, zero_index, first_frame), (1, H, extended))[0]
        delta_rows = lax.dynamic_slice(row_delta, (utterance, zero_index, first_frame), (1, H, extended))[0]
        key_pos = first_frame + jnp.arange(F, dtype=jnp.int32)
        query_pos = first_frame - W + jnp.arange(extended, dtype=jnp.int32)
        return key_side(key_rows, value_rows, query_rows, grad_rows, total_rows, delta_rows, rel_bias, key_pos, query_pos, length)

    grad_key, grad_value = lax.map(keyside_block, jnp.arange(blocks, dtype=jnp.int32))
    return context, grad_query, grad_key.reshape(BATCH, FRAMES, D), grad_value.reshape(BATCH, FRAMES, D), grad_bias
```

```python
import functools

import jax
import jax.numpy as jnp
from jax import lax
from jax.experimental import pallas as pl
from jax.experimental.pallas import tpu as pltpu
from jax.sharding import PartitionSpec as P

MESH = pl.DeviceIdType.MESH
masked_score = -1e30
lane_tile = 128
radix = 4


def sum_stages(n_dp, n_tm):
    stages = []
    stride = 1
    with_dp = True
    while stride < n_tm or with_dp:
        size = min(radix, n_tm // stride)
        stages.append((stride, size, with_dp))
        stride *= size
        with_dp = False
    return stages


def contract(left, right, left_dim, right_dim):
    return lax.dot_general(
        left, right, (((left_dim,), (right_dim,)), ((), ())), preferred_element_type=jnp.float32
    )


def kernel(
    plan,
    length_ref,
    bias_ref,
    query_hbm,
    key_hbm,
    value_hbm,
    grad_hbm,
    context_hbm,
    dquery_hbm,
    dkey_hbm,
    dvalue_hbm,
    dbias_ref,
    ext,
    own,
    bias_rows,
    bias_full,
    staged,
    key_sums,
    back_send,
    back_recv,
    diag_sums,
    tables,
    load_sem,
    store_sem,
    fwd_send_sem,
    fwd_recv_sem,
    back_send_sem,
    back_recv_sem,
    table_send_sem,
    table_recv_sem,
):
    n_dp, n_tm, heads, frames, head_size, span, chunks, chunk_lanes = plan
    extended = 3 * frames
    stages = sum_stages(n_dp, n_tm)
    dp = lax.axis_index("dp")
    tm = lax.axis_index("tm")
    has_left = tm > 0
    has_right = tm < n_tm - 1
    scaling = head_size ** (-0.5)

    def when_side(side, run):
        pl.when(has_left if side == 0 else has_right)(run)

    loads = [
        pltpu.make_async_copy(query_hbm.at[0], own.at[0], load_sem.at[0]),
        pltpu.make_async_copy(grad_hbm.at[0], own.at[1], load_sem.at[1]),
        pltpu.make_async_copy(key_hbm.at[0], ext.at[0, pl.ds(frames, frames)], load_sem.at[2]),
        pltpu.make_async_copy(value_hbm.at[0], ext.at[1, pl.ds(frames, frames)], load_sem.at[3]),
    ]
    for copy in loads:
        copy.start()

    def group_of(stage):
        stride, size, with_dp = stage
        place = lax.rem(lax.div(tm, stride), size)
        base = tm - place * stride
        total = size * (n_dp if with_dp else 1)
        mine = dp * size + place if with_dp else place

        def device(slot):
            other_dp = lax.div(slot, size) if with_dp else dp
            return (other_dp, base + lax.rem(slot, size) * stride)

        others = [lax.rem(mine + step, total) for step in range(1, total)]
        return mine, others, device, total

    groups = [group_of(stage) for stage in stages]

    barrier = pltpu.get_barrier_semaphore()

    def greet_left():
        pl.semaphore_signal(barrier, inc=1, device_id=(dp, tm - 1), device_id_type=MESH)

    def greet_right():
        pl.semaphore_signal(barrier, inc=1, device_id=(dp, tm + 1), device_id_type=MESH)

    when_side(0, greet_left)
    when_side(1, greet_right)
    greeted = 0
    for mine, others, device, total in groups:
        for slot in others:
            pl.semaphore_signal(barrier, inc=1, device_id=device(slot), device_id_type=MESH)
            greeted += 1
    neighbours = jnp.where(has_left, 1, 0) + jnp.where(has_right, 1, 0)
    pl.semaphore_wait(barrier, greeted + neighbours)

    def lanes(chunk):
        return pl.ds(chunk * chunk_lanes, chunk_lanes)

    def rim_copy(side, array, chunk):
        source = (key_hbm, value_hbm)[array].at[0, :, lanes(chunk)]
        target = ext.at[array, pl.ds(2 * frames * side, frames), lanes(chunk)]
        return pltpu.make_async_remote_copy(
            src_ref=source,
            dst_ref=target,
            send_sem=fwd_send_sem.at[side, array, chunk],
            recv_sem=fwd_recv_sem.at[side, array, chunk],
            device_id=(dp, tm + 1 - 2 * side),
            device_id_type=MESH,
        )

    def back_copy(side, chunk):
        return pltpu.make_async_remote_copy(
            src_ref=back_send.at[side, chunk],
            dst_ref=back_recv.at[side, chunk],
            send_sem=back_send_sem.at[side, chunk],
            recv_sem=back_recv_sem.at[side, chunk],
            device_id=(dp, tm - 1 + 2 * side),
            device_id_type=MESH,
        )

    for chunk in range(chunks):
        for array in (0, 1):
            for side in (0, 1):
                when_side(1 - side, lambda: rim_copy(side, array, chunk).start())

    def clear(side):
        rim = pl.ds(2 * frames * side, frames)
        for array in (0, 1):
            ext[array, rim, :] = jnp.zeros((frames, ext.shape[2]), ext.dtype)
        back_recv[1 - side] = jnp.zeros(back_recv.shape[1:], back_recv.dtype)

    pl.when(jnp.logical_not(has_left))(lambda: clear(0))
    pl.when(jnp.logical_not(has_right))(lambda: clear(1))

    length = length_ref[0]
    first = tm * frames
    row = lax.broadcasted_iota(jnp.int32, (frames, extended), 0)
    column = lax.broadcasted_iota(jnp.int32, (frames, extended), 1)
    offset = column - row
    key_pos = first - frames + column
    allowed = (offset >= 0) & (offset < span) & (key_pos >= 0) & (key_pos < length)
    bias_rows[...] = jnp.zeros_like(bias_rows)
    bias_rows[pl.ds(0, heads), pl.ds(0, span)] = bias_ref[...]
    for head in range(heads):
        spread = jnp.broadcast_to(bias_rows[pl.ds(head, 1), :], (frames, extended))
        rolled = pltpu.roll(spread, 0, 1, stride=1, stride_axis=0)
        bias_full[head] = jnp.where(allowed, rolled, masked_score)

    query_row = lax.broadcasted_iota(jnp.int32, (frames, lane_tile), 0)
    lane = lax.broadcasted_iota(jnp.int32, (frames, lane_tile), 1)
    valid = first + query_row < length
    valid_low = jnp.where(valid, 1.0, 0.0).astype(jnp.bfloat16)
    per_tile = lane_tile // head_size
    lane_head = lax.div(lane, head_size)
    picks = [jnp.where(lane_head == sub, 1.0, 0.0).astype(jnp.bfloat16) for sub in range(per_tile)]

    for copy in loads:
        copy.wait()

    stores = []

    def store(index, source, target):
        copy = pltpu.make_async_copy(source, target, store_sem.at[index])
        copy.start()
        stores.append(copy)

    for chunk in range(chunks):
        for array in (0, 1):
            for side in (0, 1):
                when_side(side, lambda: rim_copy(side, array, chunk).wait_recv())
        for tile in range(chunk_lanes // lane_tile):
            start = chunk * chunk_lanes + tile * lane_tile
            cols = pl.ds(start, lane_tile)
            first_head = start // head_size
            query = own[0, :, cols]
            grad = own[1, :, cols] * valid_low
            key = ext[0, :, cols]
            value = ext[1, :, cols]
            queries = jnp.concatenate([query * pick for pick in picks], axis=0)
            grads = jnp.concatenate([grad * pick for pick in picks], axis=0)
            rows = per_tile * frames
            bias = bias_full[pl.ds(first_head, per_tile)].reshape(rows, extended)
            scores = contract(queries, key, 1, 1) * scaling + bias
            grad_probs = contract(grads, value, 1, 1)
            top = jnp.max(scores, axis=1, keepdims=True)
            shifted = jnp.exp(scores - top)
            probs = shifted * (1.0 / jnp.sum(shifted, axis=1, keepdims=True))
            probs_low = probs.astype(jnp.bfloat16)
            delta = jnp.sum(probs * grad_probs, axis=1, keepdims=True)
            grad_scores = probs * (grad_probs - delta)
            grad_low = grad_scores.astype(jnp.bfloat16)

            dkey = contract(grad_low, queries, 0, 0)
            dvalue = contract(probs_low, grads, 0, 0)
            inner = pl.ds(tile * lane_tile, lane_tile)
            for array, part in ((0, dkey), (1, dvalue)):
                low = part.astype(jnp.bfloat16)
                back_send[0, chunk, array, :, inner] = low[:frames]
                back_send[1, chunk, array, :, inner] = low[2 * frames :]
                key_sums[array, :, cols] = part[frames : 2 * frames]

            mixed = contract(probs_low, value, 1, 0)
            dquery = contract(grad_low, key, 1, 0)
            context = mixed[:frames]
            dquery_out = dquery[:frames]
            for sub in range(1, per_tile):
                here = lane_head == sub
                context = jnp.where(here, mixed[sub * frames : (sub + 1) * frames], context)
                dquery_out = jnp.where(here, dquery[sub * frames : (sub + 1) * frames], dquery_out)
            staged[0, :, cols] = jnp.where(valid, context, 0.0).astype(jnp.bfloat16)
            staged[1, :, cols] = (dquery_out * scaling).astype(jnp.bfloat16)

            for sub in range(per_tile):
                folded = grad_scores[sub * frames : (sub + 1) * frames]
                half = frames // 2
                while half >= 8:
                    folded = folded[:half] + pltpu.roll(folded[half:], extended - half, 1)
                    half //= 2
                diag_sums[pl.ds((first_head + sub) * 8, 8), :] = folded
        for side in (0, 1):
            when_side(side, lambda: back_copy(side, chunk).start())
        store(4 * chunk, staged.at[0, :, lanes(chunk)], context_hbm.at[0, :, lanes(chunk)])
        store(4 * chunk + 1, staged.at[1, :, lanes(chunk)], dquery_hbm.at[0, :, lanes(chunk)])

    folded = diag_sums[...]
    turn = lax.rem(lax.broadcasted_iota(jnp.int32, folded.shape, 0), 8)
    for bit in (1, 2, 4):
        moved = pltpu.roll(folded, extended - bit, 1)
        folded = jnp.where(lax.rem(lax.div(turn, bit), 2) == 1, moved, folded)
    table = jnp.sum(folded.reshape(heads, 8, extended), axis=1)

    def table_copy(level, base, slot_from, slot_to, device):
        return pltpu.make_async_remote_copy(
            src_ref=tables.at[base + slot_from],
            dst_ref=tables.at[base + slot_from],
            send_sem=table_send_sem.at[base + slot_to],
            recv_sem=table_recv_sem.at[base + slot_from],
            device_id=device(slot_to),
            device_id_type=MESH,
        )

    def send_tables(level, base, table):
        mine, others, device, total = groups[level]
        tables[base + mine, pl.ds(0, heads), :] = table
        for slot in others:
            table_copy(level, base, mine, slot, device).start()

    def sum_tables(level, base):
        mine, others, device, total = groups[level]
        for slot in others:
            table_copy(level, base, slot, slot, device).wait_recv()
        whole = tables[base, pl.ds(0, heads), :]
        for slot in range(1, total):
            whole = whole + tables[base + slot, pl.ds(0, heads), :]
        return whole

    bases = []
    used = 0
    for mine, others, device, total in groups:
        bases.append(used)
        used += total

    def finish_keys():
        for chunk in range(chunks):
            for side in (0, 1):
                when_side(1 - side, lambda: back_copy(side, chunk).wait_recv())
            for array in (0, 1):
                cols = lanes(chunk)
                whole = (
                    key_sums[array, :, cols]
                    + back_recv[0, chunk, array].astype(jnp.float32)
                    + back_recv[1, chunk, array].astype(jnp.float32)
                )
                if array == 0:
                    whole = whole * scaling
                staged[2 + array, :, cols] = whole.astype(jnp.bfloat16)
                store(
                    4 * chunk + 2 + array,
                    staged.at[2 + array, :, cols],
                    (dkey_hbm, dvalue_hbm)[array].at[0, :, cols],
                )

    send_tables(0, bases[0], table)
    finish_keys()
    table = sum_tables(0, bases[0])
    for level in range(1, len(groups)):
        send_tables(level, bases[level], table)
        table = sum_tables(level, bases[level])
    dbias_ref[...] = table[:, :span]

    for level, (mine, others, device, total) in enumerate(groups):
        for slot in others:
            table_copy(level, bases[level], mine, slot, device).wait_send()
    for chunk in range(chunks):
        for side in (0, 1):
            when_side(side, lambda: back_copy(side, chunk).wait_send())
            for array in (0, 1):
                when_side(1 - side, lambda: rim_copy(side, array, chunk).wait_send())
    for copy in stores:
        copy.wait()


def on_device(n_dp, n_tm, query_proj, key_proj, value_proj, cotangent, lengths, rel_bias):
    frames, width = query_proj.shape[1:]
    heads, span = rel_bias.shape
    head_size = width // heads
    extended = 3 * frames
    chunk_lanes = 2 * lane_tile
    chunks = width // chunk_lanes
    slots = sum(size * (n_dp if with_dp else 1) for _, size, with_dp in sum_stages(n_dp, n_tm))
    plan = (n_dp, n_tm, heads, frames, head_size, span, chunks, chunk_lanes)
    block = jax.ShapeDtypeStruct((1, frames, width), jnp.bfloat16)
    low = jnp.bfloat16
    padded_heads = -(-heads // 8) * 8
    hbm = pl.BlockSpec(memory_space=pl.ANY)
    vmem = pl.BlockSpec(memory_space=pltpu.VMEM)
    return pl.pallas_call(
        functools.partial(kernel, plan),
        out_shape=(block, block, block, block, jax.ShapeDtypeStruct((heads, span), jnp.float32)),
        in_specs=[pl.BlockSpec(memory_space=pltpu.SMEM), vmem, hbm, hbm, hbm, hbm],
        out_specs=(hbm, hbm, hbm, hbm, vmem),
        scratch_shapes=[
            pltpu.VMEM((2, extended, width), low),
            pltpu.VMEM((2, frames, width), low),
            pltpu.VMEM((padded_heads, extended), jnp.float32),
            pltpu.VMEM((heads, frames, extended), jnp.float32),
            pltpu.VMEM((4, frames, width), low),
            pltpu.VMEM((2, frames, width), jnp.float32),
            pltpu.VMEM((2, chunks, 2, frames, chunk_lanes), low),
            pltpu.VMEM((2, chunks, 2, frames, chunk_lanes), low),
            pltpu.VMEM((heads * 8, extended), jnp.float32),
            pltpu.VMEM((slots, padded_heads, extended), jnp.float32),
            pltpu.SemaphoreType.DMA((4,)),
            pltpu.SemaphoreType.DMA((4 * chunks,)),
            pltpu.SemaphoreType.DMA((2, 2, chunks)),
            pltpu.SemaphoreType.DMA((2, 2, chunks)),
            pltpu.SemaphoreType.DMA((2, chunks)),
            pltpu.SemaphoreType.DMA((2, chunks)),
            pltpu.SemaphoreType.DMA((slots,)),
            pltpu.SemaphoreType.DMA((slots,)),
        ],
        compiler_params=pltpu.CompilerParams(
            collective_id=0, has_side_effects=True, vmem_limit_bytes=40 * 1024 * 1024
        ),
    )(lengths, rel_bias, query_proj, key_proj, value_proj, cotangent)


def solution(mesh):
    rows = P("dp", "tm", None)
    return jax.shard_map(
        functools.partial(on_device, mesh.shape["dp"], mesh.shape["tm"]),
        mesh=mesh,
        in_specs=(rows, rows, rows, rows, P("dp"), P()),
        out_specs=(rows, rows, rows, rows, P()),
        check_vma=False,
    )
```

```python
import functools

import jax
import jax.numpy as jnp
from jax import lax
from jax.experimental import pallas as pl
from jax.experimental.pallas import tpu as pltpu
from jax.sharding import PartitionSpec as P

MESH = pl.DeviceIdType.MESH
masked_score = -1e30
lane_tile = 128
radix = 4


def sum_stages(n_dp, n_tm):
    stages = []
    stride = 1
    with_dp = True
    while stride < n_tm or with_dp:
        size = min(radix, n_tm // stride)
        stages.append((stride, size, with_dp))
        stride *= size
        with_dp = False
    return stages


def contract(left, right, left_dim, right_dim):
    return lax.dot_general(
        left, right, (((left_dim,), (right_dim,)), ((), ())), preferred_element_type=jnp.float32
    )


def kernel(
    plan,
    length_ref,
    bias_hbm,
    query_hbm,
    key_hbm,
    value_hbm,
    grad_hbm,
    context_hbm,
    dquery_hbm,
    dkey_hbm,
    dvalue_hbm,
    dbias_hbm,
    ext,
    own,
    bias_ref,
    bias_rows,
    bias_full,
    staged,
    key_sums,
    back_send,
    back_recv,
    diag_sums,
    tables,
    load_sem,
    store_sem,
    fwd_send_sem,
    fwd_recv_sem,
    back_send_sem,
    back_recv_sem,
    table_send_sem,
    table_recv_sem,
):
    n_dp, n_tm, heads, frames, head_size, span, chunks, chunk_lanes = plan
    extended = 3 * frames
    stages = sum_stages(n_dp, n_tm)
    dp = lax.axis_index("dp")
    tm = lax.axis_index("tm")
    has_left = tm > 0
    has_right = tm < n_tm - 1
    scaling = head_size ** (-0.5)

    def when_side(side, run):
        pl.when(has_left if side == 0 else has_right)(run)

    loads = [
        pltpu.make_async_copy(query_hbm.at[0], own.at[0], load_sem.at[0]),
        pltpu.make_async_copy(grad_hbm.at[0], own.at[1], load_sem.at[1]),
        pltpu.make_async_copy(key_hbm.at[0], ext.at[0, pl.ds(frames, frames)], load_sem.at[2]),
        pltpu.make_async_copy(value_hbm.at[0], ext.at[1, pl.ds(frames, frames)], load_sem.at[3]),
    ]
    bias_load = pltpu.make_async_copy(bias_hbm, bias_ref, load_sem.at[4])
    bias_load.start()
    for copy in loads:
        copy.start()

    def group_of(stage):
        stride, size, with_dp = stage
        place = lax.rem(lax.div(tm, stride), size)
        base = tm - place * stride
        total = size * (n_dp if with_dp else 1)
        mine = dp * size + place if with_dp else place

        def device(slot):
            other_dp = lax.div(slot, size) if with_dp else dp
            return (other_dp, base + lax.rem(slot, size) * stride)

        others = [lax.rem(mine + step, total) for step in range(1, total)]
        return mine, others, device, total

    groups = [group_of(stage) for stage in stages]

    barrier = pltpu.get_barrier_semaphore()

    def greet_left():
        pl.semaphore_signal(barrier, inc=1, device_id=(dp, tm - 1), device_id_type=MESH)

    def greet_right():
        pl.semaphore_signal(barrier, inc=1, device_id=(dp, tm + 1), device_id_type=MESH)

    when_side(0, greet_left)
    when_side(1, greet_right)
    greeted = 0
    for mine, others, device, total in groups:
        for slot in others:
            pl.semaphore_signal(barrier, inc=1, device_id=device(slot), device_id_type=MESH)
            greeted += 1
    neighbours = jnp.where(has_left, 1, 0) + jnp.where(has_right, 1, 0)
    pl.semaphore_wait(barrier, greeted + neighbours)

    def lanes(chunk):
        return pl.ds(chunk * chunk_lanes, chunk_lanes)

    def rim_copy(side, array, chunk):
        source = (key_hbm, value_hbm)[array].at[0, :, lanes(chunk)]
        target = ext.at[array, pl.ds(2 * frames * side, frames), lanes(chunk)]
        return pltpu.make_async_remote_copy(
            src_ref=source,
            dst_ref=target,
            send_sem=fwd_send_sem.at[side, array, chunk],
            recv_sem=fwd_recv_sem.at[side, array, chunk],
            device_id=(dp, tm + 1 - 2 * side),
            device_id_type=MESH,
        )

    def back_copy(side, tile):
        return pltpu.make_async_remote_copy(
            src_ref=back_send.at[side, tile],
            dst_ref=back_recv.at[side, tile],
            send_sem=back_send_sem.at[side, tile],
            recv_sem=back_recv_sem.at[side, tile],
            device_id=(dp, tm - 1 + 2 * side),
            device_id_type=MESH,
        )

    for chunk in range(chunks):
        for array in (0, 1):
            for side in (0, 1):
                when_side(1 - side, lambda: rim_copy(side, array, chunk).start())

    def clear(side):
        rim = pl.ds(2 * frames * side, frames)
        for array in (0, 1):
            ext[array, rim, :] = jnp.zeros((frames, ext.shape[2]), ext.dtype)
        back_recv[1 - side] = jnp.zeros(back_recv.shape[1:], back_recv.dtype)

    pl.when(jnp.logical_not(has_left))(lambda: clear(0))
    pl.when(jnp.logical_not(has_right))(lambda: clear(1))

    length = length_ref[0]
    first = tm * frames
    row = lax.broadcasted_iota(jnp.int32, (frames, extended), 0)
    column = lax.broadcasted_iota(jnp.int32, (frames, extended), 1)
    place = column - row
    key_pos = first + frames - lax.div(column, frames) * frames + row
    allowed = (place >= 0) & (place < span) & (key_pos >= 0) & (key_pos < length)
    flip_row = lax.broadcasted_iota(jnp.int32, (extended, extended), 0)
    flip_column = lax.broadcasted_iota(jnp.int32, (extended, extended), 1)
    mirror = jnp.where(flip_row + flip_column == span - 1, 1.0, 0.0)

    def mirrored(table):
        return lax.dot_general(
            table,
            mirror,
            (((1,), (0,)), ((), ())),
            precision=lax.Precision.HIGHEST,
            preferred_element_type=jnp.float32,
        )

    per_tile = lane_tile // head_size
    bias_load.wait()
    bias_rows[...] = jnp.zeros_like(bias_rows)
    bias_rows[pl.ds(0, heads), pl.ds(0, span)] = bias_ref[...]
    bias_rows[...] = mirrored(bias_rows[...])
    for head in range(heads):
        spread = jnp.broadcast_to(bias_rows[pl.ds(head, 1), :], (frames, extended))
        rolled = pltpu.roll(spread, 0, 1, stride=1, stride_axis=0)
        masked = jnp.where(allowed, rolled, masked_score)
        for part in range(3):
            bias_full[
                head // per_tile,
                pl.ds(part * frames, frames),
                pl.ds((head % per_tile) * frames, frames),
            ] = masked[:, (2 - part) * frames : (3 - part) * frames]

    query_row = lax.broadcasted_iota(jnp.int32, (frames, lane_tile), 0)
    lane = lax.broadcasted_iota(jnp.int32, (frames, lane_tile), 1)
    valid = first + query_row < length
    valid_low = jnp.where(valid, 1.0, 0.0).astype(jnp.bfloat16)
    lane_head = lax.div(lane, head_size)
    picks = [jnp.where(lane_head == sub, 1.0, 0.0).astype(jnp.bfloat16) for sub in range(per_tile)]

    for copy in loads:
        copy.wait()

    stores = []

    def store(index, source, target):
        copy = pltpu.make_async_copy(source, target, store_sem.at[index])
        copy.start()
        stores.append(copy)

    def softmax_part(tile):
        cols = pl.ds(tile * lane_tile, lane_tile)
        query = own[0, :, cols]
        grad = own[1, :, cols] * valid_low
        key = ext[0, :, cols]
        value = ext[1, :, cols]
        queries = jnp.concatenate([query * pick for pick in picks], axis=0)
        grads = jnp.concatenate([grad * pick for pick in picks], axis=0)
        scores = contract(key, queries, 1, 1) * scaling + bias_full[tile]
        grad_probs = contract(value, grads, 1, 1)
        top = jnp.max(scores, axis=0, keepdims=True)
        shifted = jnp.exp(scores - top)
        probs = shifted * (1.0 / jnp.sum(shifted, axis=0, keepdims=True))
        probs_low = probs.astype(jnp.bfloat16)
        delta = jnp.sum(probs * grad_probs, axis=0, keepdims=True)
        grad_scores = probs * (grad_probs - delta)
        grad_low = grad_scores.astype(jnp.bfloat16)
        for sub in range(per_tile):
            mine = grad_scores[:, sub * frames : (sub + 1) * frames]
            folded = jnp.concatenate(
                [mine[part * frames : (part + 1) * frames] for part in (2, 1, 0)], axis=1
            )
            half = frames // 2
            while half >= 8:
                folded = folded[:half] + pltpu.roll(folded[half:], extended - half, 1)
                half //= 2
            diag_sums[pl.ds((tile * per_tile + sub) * 8, 8), :] = folded
        return queries, grads, probs_low, grad_low

    def product_part(tile, held):
        queries, grads, probs_low, grad_low = held
        cols = pl.ds(tile * lane_tile, lane_tile)
        key = ext[0, :, cols]
        value = ext[1, :, cols]
        for array, part in (
            (0, contract(grad_low, queries, 1, 0)),
            (1, contract(probs_low, grads, 1, 0)),
        ):
            low = part.astype(jnp.bfloat16)
            back_send[0, tile, array] = low[:frames]
            back_send[1, tile, array] = low[2 * frames :]
            key_sums[array, :, cols] = part[frames : 2 * frames]

        def own_heads(turned):
            parts = [
                turned[sub * head_size : (sub + 1) * head_size, sub * frames : (sub + 1) * frames]
                for sub in range(per_tile)
            ]
            return jnp.concatenate(parts, axis=0).T

        context = own_heads(contract(value, probs_low, 0, 0))
        dquery = own_heads(contract(key, grad_low, 0, 0))
        staged[0, :, cols] = jnp.where(valid, context, 0.0).astype(jnp.bfloat16)
        staged[1, :, cols] = (dquery * scaling).astype(jnp.bfloat16)

    def give_back(tile):
        for side in (0, 1):
            when_side(side, lambda: back_copy(side, tile).start())

    per_chunk = chunk_lanes // lane_tile
    tiles = chunks * per_chunk
    held = None
    for chunk in range(chunks):
        for array in (0, 1):
            for side in (0, 1):
                when_side(side, lambda: rim_copy(side, array, chunk).wait_recv())
        done = []
        for tile in range(chunk * per_chunk, (chunk + 1) * per_chunk):
            fresh = softmax_part(tile)
            if held is not None:
                product_part(tile - 1, held)
                done.append(tile - 1)
            held = fresh
        for tile in done:
            give_back(tile)

    folded = diag_sums[...]
    turn = lax.rem(lax.broadcasted_iota(jnp.int32, folded.shape, 0), 8)
    for bit in (1, 2, 4):
        moved = pltpu.roll(folded, extended - bit, 1)
        folded = jnp.where(lax.rem(lax.div(turn, bit), 2) == 1, moved, folded)
    table = jnp.sum(folded.reshape(heads, 8, extended), axis=1)

    def table_copy(level, base, slot_from, slot_to, device):
        return pltpu.make_async_remote_copy(
            src_ref=tables.at[base + slot_from],
            dst_ref=tables.at[base + slot_from],
            send_sem=table_send_sem.at[base + slot_to],
            recv_sem=table_recv_sem.at[base + slot_from],
            device_id=device(slot_to),
            device_id_type=MESH,
        )

    def send_tables(level, base, table):
        mine, others, device, total = groups[level]
        tables[base + mine, pl.ds(0, heads), :] = table
        for slot in others:
            table_copy(level, base, mine, slot, device).start()

    def sum_tables(level, base):
        mine, others, device, total = groups[level]
        for slot in others:
            table_copy(level, base, slot, slot, device).wait_recv()
        whole = tables[base, pl.ds(0, heads), :]
        for slot in range(1, total):
            whole = whole + tables[base + slot, pl.ds(0, heads), :]
        return whole

    bases = []
    used = 0
    for mine, others, device, total in groups:
        bases.append(used)
        used += total

    def finish_keys():
        for tile in range(tiles):
            for side in (0, 1):
                when_side(1 - side, lambda: back_copy(side, tile).wait_recv())
            for array in (0, 1):
                cols = pl.ds(tile * lane_tile, lane_tile)
                whole = (
                    key_sums[array, :, cols]
                    + back_recv[0, tile, array].astype(jnp.float32)
                    + back_recv[1, tile, array].astype(jnp.float32)
                )
                if array == 0:
                    whole = whole * scaling
                staged[2 + array, :, cols] = whole.astype(jnp.bfloat16)
        store(2, staged.at[2], dkey_hbm.at[0])
        store(3, staged.at[3], dvalue_hbm.at[0])

    send_tables(0, bases[0], table)
    product_part(tiles - 1, held)
    give_back(tiles - 1)
    store(0, staged.at[0], context_hbm.at[0])
    store(1, staged.at[1], dquery_hbm.at[0])
    table = sum_tables(0, bases[0])
    for level in range(1, len(groups)):
        send_tables(level, bases[level], table)
        if level == 1:
            finish_keys()
        table = sum_tables(level, bases[level])
    if len(groups) == 1:
        finish_keys()
    bias_rows[pl.ds(0, heads), :] = table
    bias_ref[...] = mirrored(bias_rows[...])[:heads, :span]
    store(4, bias_ref, dbias_hbm)

    for level, (mine, others, device, total) in enumerate(groups):
        for slot in others:
            table_copy(level, bases[level], mine, slot, device).wait_send()
    for side in (0, 1):
        for tile in range(tiles):
            when_side(side, lambda: back_copy(side, tile).wait_send())
        for chunk in range(chunks):
            for array in (0, 1):
                when_side(1 - side, lambda: rim_copy(side, array, chunk).wait_send())
    for copy in stores:
        copy.wait()


def on_device(n_dp, n_tm, query_proj, key_proj, value_proj, cotangent, lengths, rel_bias):
    frames, width = query_proj.shape[1:]
    heads, span = rel_bias.shape
    head_size = width // heads
    extended = 3 * frames
    chunk_lanes = 2 * lane_tile
    chunks = width // chunk_lanes
    slots = sum(size * (n_dp if with_dp else 1) for _, size, with_dp in sum_stages(n_dp, n_tm))
    plan = (n_dp, n_tm, heads, frames, head_size, span, chunks, chunk_lanes)
    block = jax.ShapeDtypeStruct((1, frames, width), jnp.bfloat16)
    low = jnp.bfloat16
    padded_heads = -(-heads // 8) * 8
    anywhere = pl.BlockSpec(memory_space=pl.ANY)
    hbm = pl.BlockSpec(memory_space=pltpu.HBM)
    tiles = width // lane_tile
    shapes = (block, block, block, block, jax.ShapeDtypeStruct((heads, span), jnp.float32))
    results = pl.pallas_call(
        functools.partial(kernel, plan),
        out_shape=shapes,
        in_specs=[pl.BlockSpec(memory_space=pltpu.SMEM)] + [hbm] * 5,
        out_specs=(anywhere,) * 5,
        scratch_shapes=[
            pltpu.VMEM((2, extended, width), low),
            pltpu.VMEM((2, frames, width), low),
            pltpu.VMEM((heads, span), jnp.float32),
            pltpu.VMEM((padded_heads, extended), jnp.float32),
            pltpu.VMEM((tiles, extended, lane_tile // head_size * frames), jnp.float32),
            pltpu.VMEM((4, frames, width), low),
            pltpu.VMEM((2, frames, width), jnp.float32),
            pltpu.VMEM((2, tiles, 2, frames, lane_tile), low),
            pltpu.VMEM((2, tiles, 2, frames, lane_tile), low),
            pltpu.VMEM((heads * 8, extended), jnp.float32),
            pltpu.VMEM((slots, padded_heads, extended), jnp.float32),
            pltpu.SemaphoreType.DMA((5,)),
            pltpu.SemaphoreType.DMA((5,)),
            pltpu.SemaphoreType.DMA((2, 2, chunks)),
            pltpu.SemaphoreType.DMA((2, 2, chunks)),
            pltpu.SemaphoreType.DMA((2, tiles)),
            pltpu.SemaphoreType.DMA((2, tiles)),
            pltpu.SemaphoreType.DMA((slots,)),
            pltpu.SemaphoreType.DMA((slots,)),
        ],
        compiler_params=pltpu.CompilerParams(
            collective_id=0, has_side_effects=True, vmem_limit_bytes=60 * 1024 * 1024
        ),
    )(lengths, rel_bias, query_proj, key_proj, value_proj, cotangent)
    return pl.pallas_call(
        hand_over,
        out_shape=shapes,
        in_specs=[anywhere] * 5,
        out_specs=(hbm,) * 5,
        scratch_shapes=[pltpu.SemaphoreType.DMA((5,))],
        compiler_params=pltpu.CompilerParams(vmem_limit_bytes=60 * 1024 * 1024),
    )(*results)


def hand_over(*refs):
    sources, targets, sems = refs[:5], refs[5:10], refs[10]
    copies = [
        pltpu.make_async_copy(source, target, sems.at[index])
        for index, (source, target) in enumerate(zip(sources, targets))
    ]
    for copy in copies:
        copy.start()
    for copy in copies:
        copy.wait()


def solution(mesh):
    rows = P("dp", "tm", None)
    return jax.shard_map(
        functools.partial(on_device, mesh.shape["dp"], mesh.shape["tm"]),
        mesh=mesh,
        in_specs=(rows, rows, rows, rows, P("dp"), P()),
        out_specs=(rows, rows, rows, rows, P()),
        check_vma=False,
    )
```

```python
import functools

import jax
import jax.numpy as jnp
from jax import lax
from jax.experimental import pallas as pl
from jax.experimental.pallas import tpu as pltpu
from jax.sharding import PartitionSpec as P

MESH = pl.DeviceIdType.MESH
masked_score = -1e30
lane_tile = 128
radix = 4


def sum_stages(n_dp, n_tm):
    stages = []
    stride = 1
    with_dp = True
    while stride < n_tm or with_dp:
        size = min(radix, n_tm // stride)
        stages.append((stride, size, with_dp))
        stride *= size
        with_dp = False
    return stages


def contract(left, right, left_dim, right_dim):
    return lax.dot_general(
        left, right, (((left_dim,), (right_dim,)), ((), ())), preferred_element_type=jnp.float32
    )


def kernel(
    plan,
    length_ref,
    bias_hbm,
    query_hbm,
    key_hbm,
    value_hbm,
    grad_hbm,
    context_hbm,
    dquery_hbm,
    dkey_hbm,
    dvalue_hbm,
    dbias_hbm,
    ext,
    own,
    bias_ref,
    bias_rows,
    bias_full,
    staged,
    key_sums,
    back_send,
    back_recv,
    diag_sums,
    tables,
    load_sem,
    store_sem,
    fwd_send_sem,
    fwd_recv_sem,
    back_send_sem,
    back_recv_sem,
    table_send_sem,
    table_recv_sem,
):
    n_dp, n_tm, heads, frames, head_size, span, chunks, chunk_lanes = plan
    extended = 3 * frames
    stages = sum_stages(n_dp, n_tm)
    dp = lax.axis_index("dp")
    tm = lax.axis_index("tm")
    has_left = tm > 0
    has_right = tm < n_tm - 1
    scaling = head_size ** (-0.5)

    def when_side(side, run):
        pl.when(has_left if side == 0 else has_right)(run)

    loads = [
        pltpu.make_async_copy(query_hbm.at[0], own.at[0], load_sem.at[0]),
        pltpu.make_async_copy(grad_hbm.at[0], own.at[1], load_sem.at[1]),
        pltpu.make_async_copy(key_hbm.at[0], ext.at[0, pl.ds(frames, frames)], load_sem.at[2]),
        pltpu.make_async_copy(value_hbm.at[0], ext.at[1, pl.ds(frames, frames)], load_sem.at[3]),
    ]
    bias_load = pltpu.make_async_copy(bias_hbm, bias_ref, load_sem.at[4])
    bias_load.start()
    for copy in loads:
        copy.start()

    def group_of(stage):
        stride, size, with_dp = stage
        place = lax.rem(lax.div(tm, stride), size)
        base = tm - place * stride
        total = size * (n_dp if with_dp else 1)
        mine = dp * size + place if with_dp else place

        def device(slot):
            other_dp = lax.div(slot, size) if with_dp else dp
            return (other_dp, base + lax.rem(slot, size) * stride)

        others = [lax.rem(mine + step, total) for step in range(1, total)]
        return mine, others, device, total

    groups = [group_of(stage) for stage in stages]

    barrier = pltpu.get_barrier_semaphore()

    def greet_left():
        pl.semaphore_signal(barrier, inc=1, device_id=(dp, tm - 1), device_id_type=MESH)

    def greet_right():
        pl.semaphore_signal(barrier, inc=1, device_id=(dp, tm + 1), device_id_type=MESH)

    when_side(0, greet_left)
    when_side(1, greet_right)
    greeted = 0
    for mine, others, device, total in groups:
        for slot in others:
            pl.semaphore_signal(barrier, inc=1, device_id=device(slot), device_id_type=MESH)
            greeted += 1
    neighbours = jnp.where(has_left, 1, 0) + jnp.where(has_right, 1, 0)
    pl.semaphore_wait(barrier, greeted + neighbours)

    def lanes(chunk):
        return pl.ds(chunk * chunk_lanes, chunk_lanes)

    def rim_copy(side, array, chunk):
        source = (key_hbm, value_hbm)[array].at[0, :, lanes(chunk)]
        target = ext.at[array, pl.ds(2 * frames * side, frames), lanes(chunk)]
        return pltpu.make_async_remote_copy(
            src_ref=source,
            dst_ref=target,
            send_sem=fwd_send_sem.at[side, array, chunk],
            recv_sem=fwd_recv_sem.at[side, array, chunk],
            device_id=(dp, tm + 1 - 2 * side),
            device_id_type=MESH,
        )

    def back_copy(side, tile):
        return pltpu.make_async_remote_copy(
            src_ref=back_send.at[side, tile],
            dst_ref=back_recv.at[side, tile],
            send_sem=back_send_sem.at[side, tile],
            recv_sem=back_recv_sem.at[side, tile],
            device_id=(dp, tm - 1 + 2 * side),
            device_id_type=MESH,
        )

    for chunk in range(chunks):
        for array in (0, 1):
            for side in (0, 1):
                when_side(1 - side, lambda: rim_copy(side, array, chunk).start())

    def clear(side):
        rim = pl.ds(2 * frames * side, frames)
        for array in (0, 1):
            ext[array, rim, :] = jnp.zeros((frames, ext.shape[2]), ext.dtype)
        back_recv[1 - side] = jnp.zeros(back_recv.shape[1:], back_recv.dtype)

    pl.when(jnp.logical_not(has_left))(lambda: clear(0))
    pl.when(jnp.logical_not(has_right))(lambda: clear(1))

    length = length_ref[0]
    first = tm * frames
    row = lax.broadcasted_iota(jnp.int32, (frames, extended), 0)
    column = lax.broadcasted_iota(jnp.int32, (frames, extended), 1)
    place = column - row
    block = jnp.where(column < frames, 1, jnp.where(column < 2 * frames, 0, -1))
    key_pos = first + block * frames + row
    allowed = (place >= 0) & (place < span) & (key_pos >= 0) & (key_pos < length)
    flip_row = lax.broadcasted_iota(jnp.int32, (extended, extended), 0)
    flip_column = lax.broadcasted_iota(jnp.int32, (extended, extended), 1)
    mirror = jnp.where(flip_row + flip_column == span - 1, 1.0, 0.0)

    def mirrored(table):
        return lax.dot_general(
            table,
            mirror,
            (((1,), (0,)), ((), ())),
            precision=lax.Precision.HIGHEST,
            preferred_element_type=jnp.float32,
        )

    per_tile = lane_tile // head_size
    bias_load.wait()
    bias_rows[...] = jnp.zeros_like(bias_rows)
    bias_rows[pl.ds(0, heads), pl.ds(0, span)] = bias_ref[...]
    bias_rows[...] = mirrored(bias_rows[...])
    spread = jnp.broadcast_to(bias_rows[pl.ds(0, heads), :][:, None, :], (heads, 8, extended))
    spread = spread.reshape(heads * 8, extended)
    turn = lax.broadcasted_iota(jnp.int32, spread.shape, 0) & 7
    for bit in (1, 2, 4):
        spread = jnp.where((turn & bit) != 0, pltpu.roll(spread, bit, 1), spread)
    for head in range(heads):
        rolled = spread[head * 8 : (head + 1) * 8]
        while rolled.shape[0] < frames:
            rolled = jnp.concatenate([rolled, pltpu.roll(rolled, rolled.shape[0], 1)], axis=0)
        masked = jnp.where(allowed, rolled, masked_score)
        for part in range(3):
            bias_full[
                head // per_tile,
                pl.ds(part * frames, frames),
                pl.ds((head % per_tile) * frames, frames),
            ] = masked[:, (2 - part) * frames : (3 - part) * frames]

    query_row = lax.broadcasted_iota(jnp.int32, (frames, lane_tile), 0)
    lane = lax.broadcasted_iota(jnp.int32, (frames, lane_tile), 1)
    valid = first + query_row < length
    valid_low = jnp.where(valid, 1.0, 0.0).astype(jnp.bfloat16)
    picks = [
        jnp.where((lane >= sub * head_size) & (lane < (sub + 1) * head_size), 1.0, 0.0).astype(
            jnp.bfloat16
        )
        for sub in range(per_tile)
    ]

    for copy in loads:
        copy.wait()

    stores = []

    def store(index, source, target):
        copy = pltpu.make_async_copy(source, target, store_sem.at[index])
        copy.start()
        stores.append(copy)

    def softmax_part(tile):
        cols = pl.ds(tile * lane_tile, lane_tile)
        query = own[0, :, cols]
        grad = own[1, :, cols] * valid_low
        key = ext[0, :, cols]
        value = ext[1, :, cols]
        queries = jnp.concatenate([query * pick for pick in picks], axis=0)
        grads = jnp.concatenate([grad * pick for pick in picks], axis=0)
        scores = contract(key, queries, 1, 1) * scaling + bias_full[tile]
        grad_probs = contract(value, grads, 1, 1)
        top = jnp.max(scores, axis=0, keepdims=True)
        shifted = jnp.exp(scores - top)
        probs = shifted * (1.0 / jnp.sum(shifted, axis=0, keepdims=True))
        probs_low = probs.astype(jnp.bfloat16)
        delta = jnp.sum(probs * grad_probs, axis=0, keepdims=True)
        grad_scores = probs * (grad_probs - delta)
        grad_low = grad_scores.astype(jnp.bfloat16)
        for sub in range(per_tile):
            mine = grad_scores[:, sub * frames : (sub + 1) * frames]
            folded = jnp.concatenate(
                [mine[part * frames : (part + 1) * frames] for part in (2, 1, 0)], axis=1
            )
            half = frames // 2
            while half >= 8:
                folded = folded[:half] + pltpu.roll(folded[half:], extended - half, 1)
                half //= 2
            diag_sums[pl.ds((tile * per_tile + sub) * 8, 8), :] = folded
        return queries, grads, probs_low, grad_low

    def product_part(tile, held):
        queries, grads, probs_low, grad_low = held
        cols = pl.ds(tile * lane_tile, lane_tile)
        key = ext[0, :, cols]
        value = ext[1, :, cols]
        for array, part in (
            (0, contract(grad_low, queries, 1, 0)),
            (1, contract(probs_low, grads, 1, 0)),
        ):
            low = part.astype(jnp.bfloat16)
            back_send[0, tile, array] = low[:frames]
            back_send[1, tile, array] = low[2 * frames :]
            key_sums[array, :, cols] = part[frames : 2 * frames]

        def own_heads(turned):
            parts = [
                turned[sub * head_size : (sub + 1) * head_size, sub * frames : (sub + 1) * frames]
                for sub in range(per_tile)
            ]
            return jnp.concatenate(parts, axis=0).T

        context = own_heads(contract(value, probs_low, 0, 0))
        dquery = own_heads(contract(key, grad_low, 0, 0))
        staged[0, :, cols] = jnp.where(valid, context, 0.0).astype(jnp.bfloat16)
        staged[1, :, cols] = (dquery * scaling).astype(jnp.bfloat16)

    def give_back(tile):
        for side in (0, 1):
            when_side(side, lambda: back_copy(side, tile).start())

    per_chunk = chunk_lanes // lane_tile
    tiles = chunks * per_chunk
    held = None
    for chunk in range(chunks):
        for array in (0, 1):
            for side in (0, 1):
                when_side(side, lambda: rim_copy(side, array, chunk).wait_recv())
        done = []
        for tile in range(chunk * per_chunk, (chunk + 1) * per_chunk):
            fresh = softmax_part(tile)
            if held is not None:
                product_part(tile - 1, held)
                done.append(tile - 1)
            held = fresh
        for tile in done:
            give_back(tile)

    folded = diag_sums[...]
    for bit in (1, 2, 4):
        moved = pltpu.roll(folded, extended - bit, 1)
        folded = jnp.where((turn & bit) != 0, moved, folded)
    table = jnp.sum(folded.reshape(heads, 8, extended), axis=1)

    def table_copy(level, base, slot_from, slot_to, device):
        return pltpu.make_async_remote_copy(
            src_ref=tables.at[base + slot_from],
            dst_ref=tables.at[base + slot_from],
            send_sem=table_send_sem.at[base + slot_to],
            recv_sem=table_recv_sem.at[base + slot_from],
            device_id=device(slot_to),
            device_id_type=MESH,
        )

    def send_tables(level, base, table):
        mine, others, device, total = groups[level]
        tables[base + mine, pl.ds(0, heads), :] = table
        for slot in others:
            table_copy(level, base, mine, slot, device).start()

    def sum_tables(level, base):
        mine, others, device, total = groups[level]
        for slot in others:
            table_copy(level, base, slot, slot, device).wait_recv()
        whole = tables[base, pl.ds(0, heads), :]
        for slot in range(1, total):
            whole = whole + tables[base + slot, pl.ds(0, heads), :]
        return whole

    bases = []
    used = 0
    for mine, others, device, total in groups:
        bases.append(used)
        used += total

    def finish_keys():
        for tile in range(tiles):
            for side in (0, 1):
                when_side(1 - side, lambda: back_copy(side, tile).wait_recv())
            for array in (0, 1):
                cols = pl.ds(tile * lane_tile, lane_tile)
                whole = (
                    key_sums[array, :, cols]
                    + back_recv[0, tile, array].astype(jnp.float32)
                    + back_recv[1, tile, array].astype(jnp.float32)
                )
                if array == 0:
                    whole = whole * scaling
                staged[2 + array, :, cols] = whole.astype(jnp.bfloat16)
        store(2, staged.at[2], dkey_hbm.at[0])
        store(3, staged.at[3], dvalue_hbm.at[0])

    send_tables(0, bases[0], table)
    product_part(tiles - 1, held)
    give_back(tiles - 1)
    store(0, staged.at[0], context_hbm.at[0])
    store(1, staged.at[1], dquery_hbm.at[0])
    table = sum_tables(0, bases[0])
    for level in range(1, len(groups)):
        send_tables(level, bases[level], table)
        if level == 1:
            finish_keys()
        table = sum_tables(level, bases[level])
    if len(groups) == 1:
        finish_keys()
    bias_rows[pl.ds(0, heads), :] = table
    bias_ref[...] = mirrored(bias_rows[...])[:heads, :span]
    store(4, bias_ref, dbias_hbm)

    for level, (mine, others, device, total) in enumerate(groups):
        for slot in others:
            table_copy(level, bases[level], mine, slot, device).wait_send()
    for side in (0, 1):
        for tile in range(tiles):
            when_side(side, lambda: back_copy(side, tile).wait_send())
        for chunk in range(chunks):
            for array in (0, 1):
                when_side(1 - side, lambda: rim_copy(side, array, chunk).wait_send())
    for copy in stores:
        copy.wait()


def on_device(n_dp, n_tm, query_proj, key_proj, value_proj, cotangent, lengths, rel_bias):
    frames, width = query_proj.shape[1:]
    heads, span = rel_bias.shape
    head_size = width // heads
    extended = 3 * frames
    chunk_lanes = 2 * lane_tile
    chunks = width // chunk_lanes
    slots = sum(size * (n_dp if with_dp else 1) for _, size, with_dp in sum_stages(n_dp, n_tm))
    plan = (n_dp, n_tm, heads, frames, head_size, span, chunks, chunk_lanes)
    block = jax.ShapeDtypeStruct((1, frames, width), jnp.bfloat16)
    low = jnp.bfloat16
    padded_heads = -(-heads // 8) * 8
    anywhere = pl.BlockSpec(memory_space=pl.ANY)
    hbm = pl.BlockSpec(memory_space=pltpu.HBM)
    tiles = width // lane_tile
    shapes = (block, block, block, block, jax.ShapeDtypeStruct((heads, span), jnp.float32))
    held_shapes = tuple(pltpu.VMEM(item.shape, item.dtype) for item in shapes)
    results = pl.pallas_call(
        functools.partial(kernel, plan),
        out_shape=held_shapes,
        in_specs=[pl.BlockSpec(memory_space=pltpu.SMEM)] + [hbm] * 5,
        out_specs=(anywhere,) * 5,
        scratch_shapes=[
            pltpu.VMEM((2, extended, width), low),
            pltpu.VMEM((2, frames, width), low),
            pltpu.VMEM((heads, span), jnp.float32),
            pltpu.VMEM((padded_heads, extended), jnp.float32),
            pltpu.VMEM((tiles, extended, lane_tile // head_size * frames), jnp.float32),
            pltpu.VMEM((4, frames, width), low),
            pltpu.VMEM((2, frames, width), jnp.float32),
            pltpu.VMEM((2, tiles, 2, frames, lane_tile), low),
            pltpu.VMEM((2, tiles, 2, frames, lane_tile), low),
            pltpu.VMEM((heads * 8, extended), jnp.float32),
            pltpu.VMEM((slots, padded_heads, extended), jnp.float32),
            pltpu.SemaphoreType.DMA((5,)),
            pltpu.SemaphoreType.DMA((5,)),
            pltpu.SemaphoreType.DMA((2, 2, chunks)),
            pltpu.SemaphoreType.DMA((2, 2, chunks)),
            pltpu.SemaphoreType.DMA((2, tiles)),
            pltpu.SemaphoreType.DMA((2, tiles)),
            pltpu.SemaphoreType.DMA((slots,)),
            pltpu.SemaphoreType.DMA((slots,)),
        ],
        compiler_params=pltpu.CompilerParams(
            collective_id=0, has_side_effects=True, vmem_limit_bytes=60 * 1024 * 1024
        ),
    )(lengths, rel_bias, query_proj, key_proj, value_proj, cotangent)
    return pl.pallas_call(
        hand_over,
        out_shape=shapes,
        in_specs=[anywhere] * 5,
        out_specs=(hbm,) * 5,
        scratch_shapes=[pltpu.SemaphoreType.DMA((5,))],
        compiler_params=pltpu.CompilerParams(vmem_limit_bytes=8 * 1024 * 1024),
    )(*results)


def hand_over(*refs):
    sources, targets, sems = refs[:5], refs[5:10], refs[10]
    copies = [
        pltpu.make_async_copy(source, target, sems.at[index])
        for index, (source, target) in enumerate(zip(sources, targets))
    ]
    for copy in copies:
        copy.start()
    for copy in copies:
        copy.wait()


def solution(mesh):
    rows = P("dp", "tm", None)
    return jax.shard_map(
        functools.partial(on_device, mesh.shape["dp"], mesh.shape["tm"]),
        mesh=mesh,
        in_specs=(rows, rows, rows, rows, P("dp"), P()),
        out_specs=(rows, rows, rows, rows, P()),
        check_vma=False,
    )
```

```python
import functools

import jax
import jax.numpy as jnp
from jax import lax
from jax.experimental import pallas as pl
from jax.experimental.pallas import tpu as pltpu
from jax.sharding import PartitionSpec as P

MESH = pl.DeviceIdType.MESH
masked_score = -1e30
lane_tile = 128
radix = 4


def sum_stages(n_dp, n_tm):
    stages = []
    stride = 1
    with_dp = True
    while stride < n_tm or with_dp:
        size = min(radix, n_tm // stride)
        stages.append((stride, size, with_dp))
        stride *= size
        with_dp = False
    return stages


def contract(left, right, left_dim, right_dim):
    return lax.dot_general(
        left, right, (((left_dim,), (right_dim,)), ((), ())), preferred_element_type=jnp.float32
    )


def kernel(
    plan,
    length_ref,
    bias_hbm,
    query_hbm,
    key_hbm,
    value_hbm,
    grad_hbm,
    context_hbm,
    dquery_hbm,
    dkey_hbm,
    dvalue_hbm,
    dbias_hbm,
    ext,
    own,
    bias_ref,
    bias_rows,
    bias_full,
    staged,
    key_sums,
    back_send,
    back_recv,
    diag_sums,
    tables,
    load_sem,
    store_sem,
    fwd_send_sem,
    fwd_recv_sem,
    back_send_sem,
    back_recv_sem,
    table_send_sem,
    table_recv_sem,
):
    n_dp, n_tm, heads, frames, head_size, span, chunks, chunk_lanes = plan
    extended = 3 * frames
    stages = sum_stages(n_dp, n_tm)
    dp = lax.axis_index("dp")
    tm = lax.axis_index("tm")
    has_left = tm > 0
    has_right = tm < n_tm - 1
    scaling = head_size ** (-0.5)

    def when_side(side, run):
        pl.when(has_left if side == 0 else has_right)(run)

    loads = [
        pltpu.make_async_copy(query_hbm.at[0], own.at[0], load_sem.at[0]),
        pltpu.make_async_copy(grad_hbm.at[0], own.at[1], load_sem.at[1]),
        pltpu.make_async_copy(key_hbm.at[0], ext.at[0, pl.ds(frames, frames)], load_sem.at[2]),
        pltpu.make_async_copy(value_hbm.at[0], ext.at[1, pl.ds(frames, frames)], load_sem.at[3]),
    ]
    bias_load = pltpu.make_async_copy(bias_hbm, bias_ref, load_sem.at[4])
    bias_load.start()
    for copy in loads:
        copy.start()

    def group_of(stage):
        stride, size, with_dp = stage
        place = lax.rem(lax.div(tm, stride), size)
        base = tm - place * stride
        total = size * (n_dp if with_dp else 1)
        mine = dp * size + place if with_dp else place

        def device(slot):
            other_dp = lax.div(slot, size) if with_dp else dp
            return (other_dp, base + lax.rem(slot, size) * stride)

        others = [lax.rem(mine + step, total) for step in range(1, total)]
        return mine, others, device, total

    groups = [group_of(stage) for stage in stages]

    barrier = pltpu.get_barrier_semaphore()

    def greet_left():
        pl.semaphore_signal(barrier, inc=1, device_id=(dp, tm - 1), device_id_type=MESH)

    def greet_right():
        pl.semaphore_signal(barrier, inc=1, device_id=(dp, tm + 1), device_id_type=MESH)

    when_side(0, greet_left)
    when_side(1, greet_right)
    greeted = 0
    for mine, others, device, total in groups:
        for slot in others:
            pl.semaphore_signal(barrier, inc=1, device_id=device(slot), device_id_type=MESH)
            greeted += 1
    neighbours = jnp.where(has_left, 1, 0) + jnp.where(has_right, 1, 0)
    pl.semaphore_wait(barrier, greeted + neighbours)

    def lanes(chunk):
        return pl.ds(chunk * chunk_lanes, chunk_lanes)

    def rim_copy(side, array, chunk):
        source = (key_hbm, value_hbm)[array].at[0, :, lanes(chunk)]
        target = ext.at[array, pl.ds(2 * frames * side, frames), lanes(chunk)]
        return pltpu.make_async_remote_copy(
            src_ref=source,
            dst_ref=target,
            send_sem=fwd_send_sem.at[side, array, chunk],
            recv_sem=fwd_recv_sem.at[side, array, chunk],
            device_id=(dp, tm + 1 - 2 * side),
            device_id_type=MESH,
        )

    def back_copy(side, tile):
        return pltpu.make_async_remote_copy(
            src_ref=back_send.at[side, tile],
            dst_ref=back_recv.at[side, tile],
            send_sem=back_send_sem.at[side, tile],
            recv_sem=back_recv_sem.at[side, tile],
            device_id=(dp, tm - 1 + 2 * side),
            device_id_type=MESH,
        )

    for chunk in range(chunks):
        for array in (0, 1):
            for side in (0, 1):
                when_side(1 - side, lambda: rim_copy(side, array, chunk).start())

    def clear(side):
        rim = pl.ds(2 * frames * side, frames)
        for array in (0, 1):
            ext[array, rim, :] = jnp.zeros((frames, ext.shape[2]), ext.dtype)
        back_recv[1 - side] = jnp.zeros(back_recv.shape[1:], back_recv.dtype)

    pl.when(jnp.logical_not(has_left))(lambda: clear(0))
    pl.when(jnp.logical_not(has_right))(lambda: clear(1))

    length = length_ref[0]
    first = tm * frames
    row = lax.broadcasted_iota(jnp.int32, (frames, extended), 0)
    column = lax.broadcasted_iota(jnp.int32, (frames, extended), 1)
    place = column - row
    block = jnp.where(column < frames, 1, jnp.where(column < 2 * frames, 0, -1))
    key_pos = first + block * frames + row
    allowed = (place >= 0) & (place < span) & (key_pos >= 0) & (key_pos < length)
    flip_row = lax.broadcasted_iota(jnp.int32, (extended, extended), 0)
    flip_column = lax.broadcasted_iota(jnp.int32, (extended, extended), 1)
    mirror = jnp.where(flip_row + flip_column == span - 1, 1.0, 0.0)

    def mirrored(table):
        return lax.dot_general(
            table,
            mirror,
            (((1,), (0,)), ((), ())),
            precision=lax.Precision.HIGHEST,
            preferred_element_type=jnp.float32,
        )

    per_tile = lane_tile // head_size
    bias_load.wait()
    bias_rows[...] = jnp.zeros_like(bias_rows)
    bias_rows[pl.ds(0, heads), pl.ds(0, span)] = bias_ref[...]
    bias_rows[...] = mirrored(bias_rows[...])
    spread = jnp.broadcast_to(bias_rows[pl.ds(0, heads), :][:, None, :], (heads, 8, extended))
    spread = spread.reshape(heads * 8, extended)
    turn = lax.broadcasted_iota(jnp.int32, spread.shape, 0) & 7
    for bit in (1, 2, 4):
        spread = jnp.where((turn & bit) != 0, pltpu.roll(spread, bit, 1), spread)
    for head in range(heads):
        rolled = spread[head * 8 : (head + 1) * 8]
        while rolled.shape[0] < frames:
            rolled = jnp.concatenate([rolled, pltpu.roll(rolled, rolled.shape[0], 1)], axis=0)
        masked = jnp.where(allowed, rolled, masked_score)
        for part in range(3):
            bias_full[
                head // per_tile,
                pl.ds(part * frames, frames),
                pl.ds((head % per_tile) * frames, frames),
            ] = masked[:, (2 - part) * frames : (3 - part) * frames]

    query_row = lax.broadcasted_iota(jnp.int32, (frames, lane_tile), 0)
    lane = lax.broadcasted_iota(jnp.int32, (frames, lane_tile), 1)
    valid = first + query_row < length
    valid_low = jnp.where(valid, 1.0, 0.0).astype(jnp.bfloat16)
    picks = [
        jnp.where((lane >= sub * head_size) & (lane < (sub + 1) * head_size), 1.0, 0.0).astype(
            jnp.bfloat16
        )
        for sub in range(per_tile)
    ]

    for copy in loads:
        copy.wait()

    stores = []

    def store(index, source, target):
        copy = pltpu.make_async_copy(source, target, store_sem.at[index])
        copy.start()
        stores.append(copy)

    def softmax_part(tile):
        cols = pl.ds(tile * lane_tile, lane_tile)
        query = own[0, :, cols]
        grad = own[1, :, cols] * valid_low
        key = ext[0, :, cols]
        value = ext[1, :, cols]
        queries = jnp.concatenate([query * pick for pick in picks], axis=0)
        grads = jnp.concatenate([grad * pick for pick in picks], axis=0)
        scores = contract(key, queries, 1, 1) * scaling + bias_full[tile]
        grad_probs = contract(value, grads, 1, 1)
        top = jnp.max(scores, axis=0, keepdims=True)
        shifted = jnp.exp(scores - top)
        probs = shifted * (1.0 / jnp.sum(shifted, axis=0, keepdims=True))
        probs_low = probs.astype(jnp.bfloat16)
        delta = jnp.sum(probs * grad_probs, axis=0, keepdims=True)
        grad_scores = probs * (grad_probs - delta)
        grad_low = grad_scores.astype(jnp.bfloat16)
        for sub in range(per_tile):
            mine = grad_scores[:, sub * frames : (sub + 1) * frames]
            folded = jnp.concatenate(
                [mine[part * frames : (part + 1) * frames] for part in (2, 1, 0)], axis=1
            )
            half = frames // 2
            while half >= 8:
                folded = folded[:half] + pltpu.roll(folded[half:], extended - half, 1)
                half //= 2
            diag_sums[pl.ds((tile * per_tile + sub) * 8, 8), :] = folded
        return queries, grads, probs_low, grad_low

    def product_part(tile, held):
        queries, grads, probs_low, grad_low = held
        cols = pl.ds(tile * lane_tile, lane_tile)
        key = ext[0, :, cols]
        value = ext[1, :, cols]
        for array, part in (
            (0, contract(grad_low, queries, 1, 0)),
            (1, contract(probs_low, grads, 1, 0)),
        ):
            low = part.astype(jnp.bfloat16)
            back_send[0, tile, array] = low[:frames]
            back_send[1, tile, array] = low[2 * frames :]
            key_sums[array, :, cols] = part[frames : 2 * frames]

        def own_heads(turned):
            parts = [
                turned[sub * head_size : (sub + 1) * head_size, sub * frames : (sub + 1) * frames]
                for sub in range(per_tile)
            ]
            return jnp.concatenate(parts, axis=0).T

        context = own_heads(contract(value, probs_low, 0, 0))
        dquery = own_heads(contract(key, grad_low, 0, 0))
        staged[0, :, cols] = jnp.where(valid, context, 0.0).astype(jnp.bfloat16)
        staged[1, :, cols] = (dquery * scaling).astype(jnp.bfloat16)

    def give_back(tile):
        for side in (0, 1):
            when_side(side, lambda: back_copy(side, tile).start())

    def table_copy(part, base, slot_from, slot_to, device):
        return pltpu.make_async_remote_copy(
            src_ref=tables.at[part, base + slot_from],
            dst_ref=tables.at[part, base + slot_from],
            send_sem=table_send_sem.at[part, base + slot_to],
            recv_sem=table_recv_sem.at[part, base + slot_from],
            device_id=device(slot_to),
            device_id_type=MESH,
        )

    parts = [(0, 8), (8, heads - 8)]

    def part_table(part):
        low_head, count = parts[part]
        folded = diag_sums[pl.ds(low_head * 8, count * 8), :]
        turn = lax.broadcasted_iota(jnp.int32, folded.shape, 0) & 7
        for bit in (1, 2, 4):
            moved = pltpu.roll(folded, extended - bit, 1)
            folded = jnp.where((turn & bit) != 0, moved, folded)
        return jnp.sum(folded.reshape(count, 8, extended), axis=1)

    def send_tables(part, level, table):
        mine, others, device, total = groups[level]
        base = bases[level]
        tables[part, base + mine, pl.ds(0, parts[part][1]), :] = table
        for slot in others:
            table_copy(part, base, mine, slot, device).start()

    def sum_tables(part, level):
        mine, others, device, total = groups[level]
        base = bases[level]
        for slot in others:
            table_copy(part, base, slot, slot, device).wait_recv()
        count = parts[part][1]
        whole = tables[part, base, pl.ds(0, count), :]
        for slot in range(1, total):
            whole = whole + tables[part, base + slot, pl.ds(0, count), :]
        return whole

    bases = []
    used = 0
    for mine, others, device, total in groups:
        bases.append(used)
        used += total

    tiles = chunks
    early = parts[0][1] // per_tile
    held = None
    for tile in range(tiles):
        for array in (0, 1):
            for side in (0, 1):
                when_side(side, lambda: rim_copy(side, array, tile).wait_recv())
        fresh = softmax_part(tile)
        if held is not None:
            product_part(tile - 1, held)
            give_back(tile - 1)
        held = fresh
        if tile == early - 1:
            send_tables(0, 0, part_table(0))

    send_tables(1, 0, part_table(1))
    product_part(tiles - 1, held)
    give_back(tiles - 1)

    def finish_keys():
        for tile in range(tiles):
            for side in (0, 1):
                when_side(1 - side, lambda: back_copy(side, tile).wait_recv())
            for array in (0, 1):
                cols = pl.ds(tile * lane_tile, lane_tile)
                whole = (
                    key_sums[array, :, cols]
                    + back_recv[0, tile, array].astype(jnp.float32)
                    + back_recv[1, tile, array].astype(jnp.float32)
                )
                if array == 0:
                    whole = whole * scaling
                staged[2 + array, :, cols] = whole.astype(jnp.bfloat16)
        store(2, staged.at[2], dkey_hbm.at[0])
        store(3, staged.at[3], dvalue_hbm.at[0])

    store(0, staged.at[0], context_hbm.at[0])
    store(1, staged.at[1], dquery_hbm.at[0])
    totals = []
    for part in (0, 1):
        totals.append(sum_tables(part, 0))
        if len(groups) > 1:
            send_tables(part, 1, totals[part])
    for level in range(1, len(groups)):
        if level == 1:
            finish_keys()
        for part in (0, 1):
            totals[part] = sum_tables(part, level)
            if level + 1 < len(groups):
                send_tables(part, level + 1, totals[part])
    if len(groups) == 1:
        finish_keys()
    for (low_head, count), total_rows in zip(parts, totals):
        bias_rows[pl.ds(low_head, count), :] = total_rows
    bias_ref[...] = mirrored(bias_rows[...])[:heads, :span]
    store(4, bias_ref, dbias_hbm)

    for level, (mine, others, device, total) in enumerate(groups):
        for slot in others:
            for part in (0, 1):
                table_copy(part, bases[level], mine, slot, device).wait_send()
    for side in (0, 1):
        for tile in range(tiles):
            when_side(side, lambda: back_copy(side, tile).wait_send())
        for chunk in range(chunks):
            for array in (0, 1):
                when_side(1 - side, lambda: rim_copy(side, array, chunk).wait_send())
    for copy in stores:
        copy.wait()


def on_device(n_dp, n_tm, query_proj, key_proj, value_proj, cotangent, lengths, rel_bias):
    frames, width = query_proj.shape[1:]
    heads, span = rel_bias.shape
    head_size = width // heads
    extended = 3 * frames
    chunk_lanes = lane_tile
    chunks = width // chunk_lanes
    slots = sum(size * (n_dp if with_dp else 1) for _, size, with_dp in sum_stages(n_dp, n_tm))
    plan = (n_dp, n_tm, heads, frames, head_size, span, chunks, chunk_lanes)
    block = jax.ShapeDtypeStruct((1, frames, width), jnp.bfloat16)
    low = jnp.bfloat16
    padded_heads = -(-heads // 8) * 8
    anywhere = pl.BlockSpec(memory_space=pl.ANY)
    hbm = pl.BlockSpec(memory_space=pltpu.HBM)
    tiles = width // lane_tile
    shapes = (block, block, block, block, jax.ShapeDtypeStruct((heads, span), jnp.float32))
    held_shapes = tuple(pltpu.VMEM(item.shape, item.dtype) for item in shapes)
    results = pl.pallas_call(
        functools.partial(kernel, plan),
        out_shape=held_shapes,
        in_specs=[pl.BlockSpec(memory_space=pltpu.SMEM)] + [hbm] * 5,
        out_specs=(anywhere,) * 5,
        scratch_shapes=[
            pltpu.VMEM((2, extended, width), low),
            pltpu.VMEM((2, frames, width), low),
            pltpu.VMEM((heads, span), jnp.float32),
            pltpu.VMEM((padded_heads, extended), jnp.float32),
            pltpu.VMEM((tiles, extended, lane_tile // head_size * frames), jnp.float32),
            pltpu.VMEM((4, frames, width), low),
            pltpu.VMEM((2, frames, width), jnp.float32),
            pltpu.VMEM((2, tiles, 2, frames, lane_tile), low),
            pltpu.VMEM((2, tiles, 2, frames, lane_tile), low),
            pltpu.VMEM((heads * 8, extended), jnp.float32),
            pltpu.VMEM((2, slots, 8, extended), jnp.float32),
            pltpu.SemaphoreType.DMA((5,)),
            pltpu.SemaphoreType.DMA((5,)),
            pltpu.SemaphoreType.DMA((2, 2, chunks)),
            pltpu.SemaphoreType.DMA((2, 2, chunks)),
            pltpu.SemaphoreType.DMA((2, tiles)),
            pltpu.SemaphoreType.DMA((2, tiles)),
            pltpu.SemaphoreType.DMA((2, slots)),
            pltpu.SemaphoreType.DMA((2, slots)),
        ],
        compiler_params=pltpu.CompilerParams(
            collective_id=0, has_side_effects=True, vmem_limit_bytes=60 * 1024 * 1024
        ),
    )(lengths, rel_bias, query_proj, key_proj, value_proj, cotangent)
    return pl.pallas_call(
        hand_over,
        out_shape=shapes,
        in_specs=[anywhere] * 5,
        out_specs=(hbm,) * 5,
        scratch_shapes=[pltpu.SemaphoreType.DMA((5,))],
        compiler_params=pltpu.CompilerParams(vmem_limit_bytes=8 * 1024 * 1024),
    )(*results)


def hand_over(*refs):
    sources, targets, sems = refs[:5], refs[5:10], refs[10]
    copies = [
        pltpu.make_async_copy(source, target, sems.at[index])
        for index, (source, target) in enumerate(zip(sources, targets))
    ]
    for copy in copies:
        copy.start()
    for copy in copies:
        copy.wait()


def solution(mesh):
    rows = P("dp", "tm", None)
    return jax.shard_map(
        functools.partial(on_device, mesh.shape["dp"], mesh.shape["tm"]),
        mesh=mesh,
        in_specs=(rows, rows, rows, rows, P("dp"), P()),
        out_specs=(rows, rows, rows, rows, P()),
        check_vma=False,
    )
```
